32 devices in a mesh: dp: 4 (over z), uly: 4 (over y, core), blk: 2 (over x).
Axes of the slice: x: 2, y: 2, z: 4, core: 2. Of those that a mesh axis runs over, the one named last changes fastest.
Arguments:
- query_rows: bfloat16 [8, 256, 3072], P(('dp', 'blk'), 'uly'), parts along dimension 0, may hold values from -400 to 400
- key_rows: bfloat16 [8, 256, 3072], P(('dp', 'blk'), 'uly'), parts along dimension 0, may hold values from -400 to 400
- value_rows: bfloat16 [8, 256, 3072], P(('dp', 'blk'), 'uly'), parts along dimension 0, may hold values from -6 to 6
- norm_query: float32 [3072], replicated, may hold values from 1 to 2.2
- norm_key: float32 [3072], replicated, may hold values from 1 to 2.2
- out_weight: bfloat16 [3072, 5120], P('blk', 'uly'), may hold values from -0.109375 to 0.109375
- out_bias: float32 [5120], P('uly'), may hold values from -3 to 3
- gate: float32 [5120], P('uly'), may hold values from 0.3 to 1.5
- residual: bfloat16 [8, 256, 5120], P(('dp', 'blk'), None, 'uly'), parts along dimension 0, may hold values from -3 to 3
Outputs:
- mixed: bfloat16 [8, 256, 5120], P(('dp', 'blk'), None, 'uly'), parts along dimension 0
The draws below stay inside these ranges and needn't reach their ends.
There are 4 independent parts, one for each index of `dp`. The reference program is written for one: setup_inputs(seed, part) draws one part's arguments, and reference() takes and returns one part's arrays. A program takes and returns all parts, laid end to end along the dimension named above; an argument that names none is the same for every part. Nothing has to cross between parts.
All inputs are finite; a program needn't handle non-finite values.
Results may differ from the reference program's by a relative error of at most 0.011.
Values may be sent and summed in bfloat16 or wider, within the bound.
A program may use at most 64 MiB of HBM per device.

```python
import math
import jax
import jax.numpy as jnp
from jax import lax

D = 5120
HEADS = 24
HEAD = 128
HD = 3072
BLOCK = 256
SEQ = 512
N_BLK = 2


def common_parts(key):
    scales = jnp.exp(jax.random.uniform(jax.random.fold_in(key, 2), (HD,), jnp.float32) * math.log(10.0))
    return scales


def own_rows(key, salt):
    base = jnp.clip(jax.random.normal(jax.random.fold_in(key, salt), (SEQ, HD), jnp.float32), -4.0, 4.0)
    row_scale = jnp.exp(jax.random.uniform(jax.random.fold_in(key, salt + 1), (SEQ, 1), jnp.float32) * math.log(10.0))
    return (base, row_scale)


def draw_query_rows(key, part):
    scales = common_parts(key)
    base, row_scale = own_rows(key, 11)
    drawn = base * row_scale * scales
    return drawn.reshape(N_BLK, BLOCK, HD).astype(jnp.bfloat16)


def draw_key_rows(key, part):
    scales = common_parts(key)
    base, row_scale = own_rows(key, 21)
    drawn = base * row_scale * scales
    return drawn.reshape(N_BLK, BLOCK, HD).astype(jnp.bfloat16)


def block_levels(key, shape, cuts, smallest, largest):
    factor_of = 1.0
    for axis_at, shards_of in cuts:
        draws = jax.random.uniform(jax.random.fold_in(jax.random.fold_in(key, 6), axis_at), (shards_of,), jnp.float32, smallest / len(cuts), largest / len(cuts))
        factor_of = factor_of * jnp.repeat(jnp.exp(draws), shape[axis_at] // shards_of).reshape((-1,) + (1,) * (len(shape) - 1 - axis_at))
    return factor_of


def centred(stream_key, extent, spread, most, pieces=(), kind=jnp.bfloat16):
    result = spread * jax.random.normal(stream_key, extent, jnp.float32)
    if pieces:
        result = result * block_levels(stream_key, extent, pieces, -0.22, 0.18)
    return jnp.clip(result, -most, most).astype(kind)


def setup_inputs(seed: int = 0, part: int = 0) -> dict:
    key_list = jax.random.split(jax.random.key(seed), 10)
    part_keys = jax.random.split(jax.random.fold_in(key_list[9], part), 10)
    return {
        "query_rows": draw_query_rows(jax.random.fold_in(jax.random.fold_in(key_list[9], part), 71), part),
        "key_rows": draw_key_rows(jax.random.fold_in(jax.random.fold_in(key_list[9], part), 71), part),
        "value_rows": centred(part_keys[2], (N_BLK, BLOCK, HD), 1.0, 6.0, ((0, 2), (1, 4))),
        "norm_query": jnp.clip(jnp.exp(jax.random.uniform(key_list[3], (HD,), jnp.float32, math.log(1.0), math.log(2.2))), 1.0, 2.2),
        "norm_key": jnp.clip(jnp.exp(jax.random.uniform(key_list[4], (HD,), jnp.float32, math.log(1.0), math.log(2.2))), 1.0, 2.2),
        "out_weight": centred(key_list[5], (HD, D), HD ** -0.5, 0.109375, ((0, 2), (1, 4))),
        "out_bias": centred(key_list[6], (D,), 0.5, 3.0, ((0, 4),), jnp.float32),
        "gate": jnp.clip(0.3 + 1.2 * jax.random.uniform(key_list[7], (D,), jnp.float32) ** block_levels(key_list[7], (D,), ((0, 4),), -0.2, 0.2), 0.3, 1.5),
        "residual": centred(part_keys[8], (N_BLK, BLOCK, D), 0.5, 3.0, ((0, 2), (2, 4))),
    }


EPS = 1e-06

def normalize(rows_in, gain):
    wide = rows_in.astype(jnp.float32)
    factor = lax.rsqrt(lax.optimization_barrier(jnp.mean(wide * wide, axis=-1, keepdims=True)) + EPS)
    return (wide * factor * gain).astype(jnp.bfloat16)

def one_head(triple):
    queries, keys, values = triple
    scores = jnp.dot(queries, keys.T, preferred_element_type=jnp.float32) * HEAD ** (-0.5)
    peak = lax.optimization_barrier(jnp.max(scores, axis=1, keepdims=True))
    weights = jnp.exp(scores - peak)
    total = lax.optimization_barrier(jnp.sum(weights, axis=1, keepdims=True))
    numer = jnp.dot(weights.astype(jnp.bfloat16), values, preferred_element_type=jnp.float32)
    return (numer / total).astype(jnp.bfloat16)

def flatten(array):
    return array.reshape(SEQ, array.shape[-1])

def split_heads(array):
    return array.reshape(SEQ, HEADS, HEAD).transpose(1, 0, 2)

def reference(query_rows, key_rows, value_rows, norm_query, norm_key, out_weight, out_bias, gate, residual):
    query_norm = normalize(flatten(query_rows), norm_query)
    key_norm = normalize(flatten(key_rows), norm_key)
    values = flatten(value_rows)
    attended = lax.map(one_head, (split_heads(query_norm), split_heads(key_norm), split_heads(values)))
    attended = attended.transpose(1, 0, 2).reshape(SEQ, HD)
    projected = jnp.dot(attended, out_weight, preferred_element_type=jnp.float32)
    mixed = flatten(residual).astype(jnp.float32) + gate * (projected + out_bias)
    return mixed.astype(jnp.bfloat16).reshape(N_BLK, BLOCK, D)
```

```python
import functools

import jax
import jax.numpy as jnp
from jax import lax
from jax.experimental import pallas as pl
from jax.experimental.pallas import tpu as pltpu
from jax.sharding import PartitionSpec as P

HEAD = 128
EPS = 1e-06
MESH = pl.DeviceIdType.MESH
LOG2E = 1.4426950408889634


def normalize_rows(rows_ref, gain_ref):
    count = rows_ref.shape[0]
    step = 16

    def visit(i, carry):
        at = pl.ds(pl.multiple_of(i * step, step), step)
        wide = rows_ref[at, :].astype(jnp.float32)
        factor = lax.rsqrt(jnp.mean(wide * wide, axis=-1, keepdims=True) + EPS)
        rows_ref[at, :] = (wide * factor * gain_ref[...]).astype(jnp.bfloat16)
        return carry

    lax.fori_loop(0, count // step, visit, 0)


def fused_kernel(
    n_u,
    q_hbm, k_hbm, v_hbm, nq_hbm, nk_hbm, w_hbm, bias_hbm, gate_hbm, res_hbm,
    out_hbm,
    q_in, k_in, nq, nk, w, bias, gate, res,
    q_all, k_all, v_all, att, acc, sent, received, result,
    load_sem, own_sem, out_sem, send_sem, recv_sem, att_send, att_recv, fwd_send, fwd_recv, sum_send, sum_recv,
):
    u = lax.axis_index("uly")
    b = lax.axis_index("blk")
    other = 1 - b
    rows = q_in.shape[0]
    wide = q_all.shape[1]
    heads = wide // HEAD
    block = rows * n_u
    columns = w.shape[1]
    tile = 256 if columns % 256 == 0 else 128
    tiles = columns // tile
    sibling = u + 1 - 2 * lax.rem(u, 2)

    peers = [(1, du) for du in range(n_u)] + [(0, du) for du in range(1, n_u)]

    def peer_id(db, du):
        return {"uly": lax.rem(u + du, n_u), "blk": other if db else b}

    barrier = pltpu.get_barrier_semaphore()
    for db, du in peers:
        pl.semaphore_signal(barrier, inc=1, device_id=peer_id(db, du), device_id_type=MESH)

    loads = [
        pltpu.make_async_copy(source, target, load_sem.at[i])
        for i, (source, target) in enumerate(
            (
                (k_hbm.at[0], k_in),
                (nk_hbm, nk),
                (q_hbm.at[0], q_in),
                (nq_hbm, nq),
                (w_hbm, w),
                (bias_hbm, bias),
                (gate_hbm, gate),
                (res_hbm.at[0], res),
            )
        )
    ]
    for load in loads[:4]:
        load.start()

    def spread(index, source, target):
        copies = []
        for db, du in peers:
            to = peer_id(db, du)
            start = pl.multiple_of((to["blk"] * n_u + to["uly"]) * wide, HEAD)
            at = pl.multiple_of((0 if db else block) + u * rows, rows)
            copy = pltpu.make_async_remote_copy(
                src_ref=source.at[:, pl.ds(start, wide)],
                dst_ref=target.at[pl.ds(at, rows), :],
                send_sem=send_sem.at[index, db * n_u + du],
                recv_sem=recv_sem.at[index, db * n_u + du],
                device_id=to,
                device_id_type=MESH,
            )
            copy.start()
            copies.append(copy)
        mine = pltpu.make_async_copy(
            source.at[:, pl.ds(pl.multiple_of((b * n_u + u) * wide, HEAD), wide)],
            target.at[pl.ds(pl.multiple_of(block + u * rows, rows), rows), :],
            own_sem.at[index],
        )
        mine.start()
        return copies, mine

    pl.semaphore_wait(barrier, len(peers))
    v_copies, v_mine = spread(0, v_hbm.at[0], v_all)
    loads[0].wait()
    loads[1].wait()
    normalize_rows(k_in, nk)
    k_copies, k_mine = spread(1, k_in, k_all)
    loads[2].wait()
    loads[3].wait()
    normalize_rows(q_in, nq)
    q_copies, q_mine = spread(2, q_in, q_all)
    for load in loads[4:]:
        load.start()

    for copy in v_copies + k_copies + q_copies[:n_u]:
        copy.wait_recv()
    v_mine.wait()
    k_mine.wait()

    scale = HEAD ** (-0.5) * LOG2E

    def attend(slot, h):
        feature = pl.ds(h * HEAD, HEAD)
        scores = lax.dot_general(
            q_all[pl.ds(slot * block, block), feature],
            k_all[:, feature],
            (((1,), (1,)), ((), ())),
            preferred_element_type=jnp.float32,
        )
        peak = jnp.max(scores, axis=1, keepdims=True)
        weights = jnp.exp2((scores - peak) * scale)
        total = jnp.sum(weights, axis=1, keepdims=True)
        numer = jnp.dot(weights.astype(jnp.bfloat16), v_all[:, feature], preferred_element_type=jnp.float32)
        at = pl.multiple_of(u * wide + h * HEAD, HEAD)
        att[pl.ds(slot * block, block), pl.ds(at, HEAD)] = (numer / total).astype(jnp.bfloat16)

    chips = n_u // 2
    pair = [2 * i for i in range(1, chips)]

    def share(slot, h):
        at = pl.multiple_of(u * wide + h * HEAD, HEAD)
        place = att.at[pl.ds(slot * block, block), pl.ds(at, HEAD)]
        copies = []
        for i, du in enumerate(pair + [None]):
            to = {"uly": sibling if du is None else lax.rem(u + du, n_u)}
            copy = pltpu.make_async_remote_copy(
                src_ref=place,
                dst_ref=place,
                send_sem=att_send.at[slot, h, i],
                recv_sem=att_recv.at[slot, h, i],
                device_id=to,
                device_id_type=MESH,
            )
            copy.start()
            copies.append(copy)
        return copies

    def forward(slot, h, shared):
        copies = []
        for i, du in enumerate(pair):
            shared[i].wait_recv()
            origin = lax.rem(u + n_u - du, n_u)
            at = pl.multiple_of(origin * wide + h * HEAD, HEAD)
            place = att.at[pl.ds(slot * block, block), pl.ds(at, HEAD)]
            copy = pltpu.make_async_remote_copy(
                src_ref=place,
                dst_ref=place,
                send_sem=fwd_send.at[slot, h, i],
                recv_sem=fwd_recv.at[slot, h, i],
                device_id={"uly": sibling},
                device_id_type=MESH,
            )
            copy.start()
            copies.append(copy)
        return copies

    shared, forwarded = {}, {}
    for h in range(heads):
        attend(0, h)
        shared[0, h] = share(0, h)
    for copy in q_copies[n_u:]:
        copy.wait_recv()
    q_mine.wait()
    for h in range(heads):
        attend(1, h)
        shared[1, h] = share(1, h)

    for load in loads[4:]:
        load.wait()

    def gathered(slot):
        for h in range(heads):
            forwarded[slot, h] = forward(slot, h, shared[slot, h])
        for h in range(heads):
            shared[slot, h][-1].wait_recv()
        for h in range(heads):
            for copy in forwarded[slot, h]:
                copy.wait_recv()

    def sum_copy(j):
        at = pl.ds(pl.multiple_of(j * tile, tile), tile)
        return pltpu.make_async_remote_copy(
            src_ref=sent.at[:, at],
            dst_ref=received.at[:, at],
            send_sem=sum_send.at[j],
            recv_sem=sum_recv.at[j],
            device_id={"blk": other},
            device_id_type=MESH,
        )

    def out_copy(j):
        at = pl.ds(pl.multiple_of(j * tile, tile), tile)
        return pltpu.make_async_copy(result.at[:, at], out_hbm.at[0, :, at], out_sem.at[j])

    gathered(0)

    def project_other(j, carry):
        at = pl.ds(pl.multiple_of(j * tile, tile), tile)
        product = jnp.dot(att[:block, :], w[:, at], preferred_element_type=jnp.float32)
        sent[:, at] = product.astype(jnp.bfloat16)
        sum_copy(j).start()
        return carry

    lax.fori_loop(0, tiles, project_other, 0)

    gathered(1)

    def project_own(j, carry):
        at = pl.ds(pl.multiple_of(j * tile, tile), tile)
        product = jnp.dot(att[block:, :], w[:, at], preferred_element_type=jnp.float32)
        acc[:, at] = res[:, at].astype(jnp.float32) + gate[:, at] * (product + bias[:, at])
        return carry

    lax.fori_loop(0, tiles, project_own, 0)

    def finish(j, carry):
        at = pl.ds(pl.multiple_of(j * tile, tile), tile)
        sum_copy(j).wait_recv()
        result[:, at] = (acc[:, at] + gate[:, at] * received[:, at].astype(jnp.float32)).astype(jnp.bfloat16)
        out_copy(j).start()
        return carry

    lax.fori_loop(0, tiles, finish, 0)

    for copy in v_copies + k_copies + q_copies:
        copy.wait_send()
    for copies in list(shared.values()) + list(forwarded.values()):
        for copy in copies:
            copy.wait_send()

    def drain(j, carry):
        sum_copy(j).wait_send()
        out_copy(j).wait()
        return carry

    lax.fori_loop(0, tiles, drain, 0)


def fused_shards(n_u, n_b, q, k, v, norm_query, norm_key, out_weight, out_bias, gate, residual):
    rows, features = q.shape[1:]
    depth, columns = out_weight.shape
    wide = features // (n_u * n_b)
    heads = wide // HEAD
    block = rows * n_u
    seq = block * n_b
    tiles = columns // (256 if columns % 256 == 0 else 128)
    chips = n_u // 2
    bf16, f32 = jnp.bfloat16, jnp.float32
    dma = pltpu.SemaphoreType.DMA
    return pl.pallas_call(
        functools.partial(fused_kernel, n_u),
        out_shape=jax.ShapeDtypeStruct(residual.shape, bf16),
        in_specs=[pl.BlockSpec(memory_space=pl.ANY)] * 9,
        out_specs=pl.BlockSpec(memory_space=pl.ANY),
        scratch_shapes=[
            pltpu.VMEM((rows, features), bf16),
            pltpu.VMEM((rows, features), bf16),
            pltpu.VMEM((1, features), f32),
            pltpu.VMEM((1, features), f32),
            pltpu.VMEM((depth, columns), bf16),
            pltpu.VMEM((1, columns), f32),
            pltpu.VMEM((1, columns), f32),
            pltpu.VMEM((block, columns), bf16),
            pltpu.VMEM((seq, wide), bf16),
            pltpu.VMEM((seq, wide), bf16),
            pltpu.VMEM((seq, wide), bf16),
            pltpu.VMEM((seq, depth), bf16),
            pltpu.VMEM((block, columns), f32),
            pltpu.VMEM((block, columns), bf16),
            pltpu.VMEM((block, columns), bf16),
            pltpu.VMEM((block, columns), bf16),
            dma((8,)),
            dma((3,)),
            dma((tiles,)),
            dma((3, 2 * n_u)),
            dma((3, 2 * n_u)),
            dma((2, heads, chips)),
            dma((2, heads, chips)),
            dma((2, heads, max(chips - 1, 1))),
            dma((2, heads, max(chips - 1, 1))),
            dma((tiles,)),
            dma((tiles,)),
        ],
        compiler_params=pltpu.CompilerParams(
            collective_id=0, has_side_effects=True, vmem_limit_bytes=48 * 1024 * 1024
        ),
    )(
        q, k, v,
        norm_query.reshape(1, features), norm_key.reshape(1, features),
        out_weight,
        out_bias.reshape(1, columns), gate.reshape(1, columns),
        residual,
    )


def normalize(rows_in, gain):
    wide = rows_in.astype(jnp.float32)
    factor = lax.rsqrt(jnp.mean(wide * wide, axis=-1, keepdims=True) + EPS)
    return (wide * factor * gain).astype(jnp.bfloat16)


def split_heads(array):
    return array.reshape(array.shape[0], array.shape[1] // HEAD, HEAD)


def initial_state(queries):
    count = queries.shape[1]
    length = queries.shape[0]
    return (
        jnp.full((count, length), -1e30, jnp.float32),
        jnp.zeros((count, length), jnp.float32),
        jnp.zeros((count, length, HEAD), jnp.float32),
    )


def absorb(state, keys, values, queries):
    peak, total, accum = state
    scores = jnp.einsum(
        "qhd,khd->hqk", queries, keys, preferred_element_type=jnp.float32
    ) * HEAD ** (-0.5)
    new_peak = jnp.maximum(peak, jnp.max(scores, axis=2))
    factor = jnp.exp(peak - new_peak)
    weights = jnp.exp(scores - new_peak[:, :, None])
    total = total * factor + jnp.sum(weights, axis=2)
    accum = accum * factor[:, :, None] + jnp.einsum(
        "hqk,khd->hqd", weights.astype(jnp.bfloat16), values, preferred_element_type=jnp.float32
    )
    return (new_peak, total, accum)


def attend_blocks(state, keys, values, queries):
    length = keys.shape[0]
    stride = 512
    count = keys.shape[1] // HEAD
    key_blocks = keys.reshape(length // stride, stride, count, HEAD)
    value_blocks = values.reshape(length // stride, stride, count, HEAD)

    def visit(carry, pair):
        return (absorb(carry, pair[0], pair[1], queries), None)

    state, unused = lax.scan(visit, state, (key_blocks, value_blocks))
    return state


def general_shards(
    query_rows, key_rows, value_rows, norm_query, norm_key, out_weight, out_bias, gate, residual
):
    local_query = normalize(query_rows[0], norm_query)
    local_key = normalize(key_rows[0], norm_key)
    local_value = value_rows[0]
    head_query = lax.all_to_all(local_query, "uly", split_axis=1, concat_axis=0, tiled=True)
    head_key, head_value = (
        lax.all_to_all(local_key, "uly", split_axis=1, concat_axis=0, tiled=True),
        lax.all_to_all(local_value, "uly", split_axis=1, concat_axis=0, tiled=True),
    )
    queries = split_heads(head_query)
    state = attend_blocks(
        initial_state(queries),
        lax.all_gather(head_key, "blk", axis=0, tiled=True),
        lax.all_gather(head_value, "blk", axis=0, tiled=True),
        queries,
    )
    peak, total, accum = state
    length = queries.shape[0]
    attended = (accum / total[:, :, None]).astype(jnp.bfloat16)
    attended = attended.transpose(1, 0, 2).reshape(length, queries.shape[1] * HEAD)
    gathered = lax.all_gather(attended, "uly", axis=1, tiled=True)
    projected = jnp.dot(
        gathered,
        lax.all_gather(out_weight, "blk", axis=0, tiled=True),
        preferred_element_type=jnp.float32,
    )
    mixed = residual[0].astype(jnp.float32) + gate * (projected + out_bias)
    return mixed.astype(jnp.bfloat16)[None]


def solution(mesh):
    n_u, n_b = mesh.shape["uly"], mesh.shape["blk"]
    placed = (
        P(("dp", "blk"), "uly", None),
        P(("dp", "blk"), "uly", None),
        P(("dp", "blk"), "uly", None),
        P(),
        P(),
        P("blk", "uly"),
        P("uly"),
        P("uly"),
        P(("dp", "blk"), None, "uly"),
    )

    def shards(query_rows, *rest):
        heads = query_rows.shape[2] // HEAD
        if n_b == 2 and n_u % 2 == 0 and heads % (n_u * n_b) == 0:
            return fused_shards(n_u, n_b, query_rows, *rest)
        return general_shards(query_rows, *rest)

    return jax.shard_map(
        shards, mesh=mesh, in_specs=placed, out_specs=P(("dp", "blk"), None, "uly"), check_vma=False
    )
```

```python
import functools

import jax
import jax.numpy as jnp
from jax import lax
from jax.experimental import pallas as pl
from jax.experimental.pallas import tpu as pltpu
from jax.sharding import PartitionSpec as P

HEAD = 128
EPS = 1e-06
MESH = pl.DeviceIdType.MESH
LOG2E = 1.4426950408889634


def normalize_rows(rows_ref, gain_ref):
    count = rows_ref.shape[0]
    step = 16

    def visit(i, carry):
        at = pl.ds(pl.multiple_of(i * step, step), step)
        wide = rows_ref[at, :].astype(jnp.float32)
        factor = lax.rsqrt(jnp.mean(wide * wide, axis=-1, keepdims=True) + EPS)
        rows_ref[at, :] = (wide * factor * gain_ref[...]).astype(jnp.bfloat16)
        return carry

    lax.fori_loop(0, count // step, visit, 0)


def fused_kernel(
    n_u, parts,
    q_hbm, k_hbm, v_hbm, nq_hbm, nk_hbm, w_hbm, bias_hbm, gate_hbm, res_hbm,
    out_hbm,
    q_in, k_in, nq, nk, w, bias_line, gate_line, res, bias, gate,
    q_all, k_all, v_all, att, acc, sent, received, result,
    load_sem, own_sem, out_sem, send_sem, recv_sem, q_send, q_recv, att_send, att_recv, fwd_send, fwd_recv, sum_send, sum_recv,
):
    u = lax.axis_index("uly")
    b = lax.axis_index("blk")
    other = 1 - b
    rows = q_in.shape[0]
    wide = q_all.shape[1]
    heads = wide // HEAD
    block = rows * n_u
    columns = w.shape[1]
    tile = 256 if columns % 256 == 0 else 128
    tiles = columns // tile
    sibling = u + 1 - 2 * lax.rem(u, 2)

    peers = [(1, du) for du in range(n_u)] + [(0, du) for du in range(1, n_u)]

    def peer_id(db, du):
        return {"uly": lax.rem(u + du, n_u), "blk": other if db else b}

    barrier = pltpu.get_barrier_semaphore()
    for db, du in peers:
        pl.semaphore_signal(barrier, inc=1, device_id=peer_id(db, du), device_id_type=MESH)

    loads = [
        pltpu.make_async_copy(source, target, load_sem.at[i])
        for i, (source, target) in enumerate(
            (
                (k_hbm.at[0], k_in),
                (nk_hbm, nk),
                (q_hbm.at[0], q_in),
                (nq_hbm, nq),
                (w_hbm, w),
                (bias_hbm, bias_line),
                (gate_hbm, gate_line),
                (res_hbm.at[0], res),
            )
        )
    ]
    for load in loads[:4]:
        load.start()

    def place_copy(source, target, db, du, first, count, at, send, recv):
        to = peer_id(db, du)
        start = pl.multiple_of((to["blk"] * n_u + to["uly"]) * wide, HEAD)
        copy = pltpu.make_async_remote_copy(
            src_ref=source.at[pl.ds(first, count), pl.ds(start, wide)],
            dst_ref=target.at[pl.ds(at, count), :],
            send_sem=send,
            recv_sem=recv,
            device_id=to,
            device_id_type=MESH,
        )
        copy.start()
        return copy

    def keep(index, source, target):
        copy = pltpu.make_async_copy(
            source.at[:, pl.ds(pl.multiple_of((b * n_u + u) * wide, HEAD), wide)],
            target.at[pl.ds(pl.multiple_of(block + u * rows, rows), rows), :],
            own_sem.at[index],
        )
        copy.start()
        return copy

    def spread(index, source, target, some):
        return [
            place_copy(
                source, target, db, du, 0, rows, pl.multiple_of((0 if db else block) + u * rows, rows),
                send_sem.at[index, db * n_u + du], recv_sem.at[index, db * n_u + du],
            )
            for db, du in some
        ]

    piece = rows // parts
    span = piece * n_u

    def spread_part(c):
        return [
            place_copy(
                q_in, q_all, 1, du, c * piece, piece, pl.multiple_of(c * span + u * piece, piece),
                q_send.at[c, du], q_recv.at[c, du],
            )
            for du in range(n_u)
        ]

    pl.semaphore_wait(barrier, len(peers))
    v_copies = spread(0, v_hbm.at[0], v_all, peers)
    v_mine = keep(0, v_hbm.at[0], v_all)
    loads[0].wait()
    loads[1].wait()
    normalize_rows(k_in, nk)
    k_copies = spread(1, k_in, k_all, peers)
    k_mine = keep(1, k_in, k_all)
    loads[2].wait()
    loads[3].wait()
    normalize_rows(q_in, nq)
    part_copies = [spread_part(0)]
    for load in loads[4:]:
        load.start()

    for copy in v_copies + k_copies:
        copy.wait_recv()
    v_mine.wait()
    k_mine.wait()
    for c in range(1, parts):
        part_copies.append(spread_part(c))
    q_copies = spread(2, q_in, q_all, peers[n_u:])
    q_mine = keep(2, q_in, q_all)

    scale = HEAD ** (-0.5) * LOG2E
    sections = [(c * span, span) for c in range(parts)] + [(block, block)]

    def attend(section):
        first, count = sections[section]
        for h in range(heads):
            feature = pl.ds(h * HEAD, HEAD)
            scores = lax.dot_general(
                q_all[pl.ds(first, count), feature],
                k_all[:, feature],
                (((1,), (1,)), ((), ())),
                preferred_element_type=jnp.float32,
            )
            peak = jnp.max(scores, axis=1, keepdims=True)
            weights = jnp.exp2((scores - peak) * scale)
            total = jnp.sum(weights, axis=1, keepdims=True)
            numer = jnp.dot(weights.astype(jnp.bfloat16), v_all[:, feature], preferred_element_type=jnp.float32)
            at = pl.multiple_of(u * wide + h * HEAD, HEAD)
            att[pl.ds(first, count), pl.ds(at, HEAD)] = (numer / total).astype(jnp.bfloat16)

    chips = n_u // 2
    pair = [2 * i for i in range(1, chips)]
    shared, forwarded = {}, {}

    def pass_on(section, origin, to, send, recv):
        first, count = sections[section]
        place = att.at[pl.ds(first, count), pl.ds(pl.multiple_of(origin * wide, HEAD), wide)]
        copy = pltpu.make_async_remote_copy(
            src_ref=place, dst_ref=place, send_sem=send, recv_sem=recv, device_id={"uly": to}, device_id_type=MESH
        )
        copy.start()
        return copy

    def share(section):
        shared[section] = [
            pass_on(section, u, to, att_send.at[section, i], att_recv.at[section, i])
            for i, to in enumerate([lax.rem(u + du, n_u) for du in pair] + [sibling])
        ]

    def gather(section):
        forwarded[section] = []
        for i, du in enumerate(pair):
            shared[section][i].wait_recv()
            origin = lax.rem(u + n_u - du, n_u)
            forwarded[section].append(
                pass_on(section, origin, sibling, fwd_send.at[section, i], fwd_recv.at[section, i])
            )
        shared[section][-1].wait_recv()
        for copy in forwarded[section]:
            copy.wait_recv()

    def columns_of(j):
        return pl.ds(pl.multiple_of(j * tile, tile), tile)

    def sum_copy(c, j):
        place = (pl.ds(c * span, span), columns_of(j))
        return pltpu.make_async_remote_copy(
            src_ref=sent.at[place],
            dst_ref=received.at[place],
            send_sem=sum_send.at[c, j],
            recv_sem=sum_recv.at[c, j],
            device_id={"blk": other},
            device_id_type=MESH,
        )

    def out_copy(j):
        return pltpu.make_async_copy(result.at[:, columns_of(j)], out_hbm.at[0, :, columns_of(j)], out_sem.at[j])

    def project_part(c):
        def visit(j, carry):
            product = jnp.dot(
                att[pl.ds(c * span, span), :], w[:, columns_of(j)], preferred_element_type=jnp.float32
            )
            sent[pl.ds(c * span, span), columns_of(j)] = product.astype(jnp.bfloat16)
            sum_copy(c, j).start()
            return carry

        lax.fori_loop(0, tiles, visit, 0)

    def attend_own():
        for copy in q_copies:
            copy.wait_recv()
        q_mine.wait()
        attend(parts)
        share(parts)

    for c in range(parts):
        for copy in part_copies[c]:
            copy.wait_recv()
        attend(c)
        share(c)

    for load in loads[4:]:
        load.wait()
    bias[...] = bias_line[...].reshape(1, columns)
    gate[...] = gate_line[...].reshape(1, columns)

    for c in range(parts):
        gather(c)
        project_part(c)
        if c == 0:
            attend_own()
    gather(parts)

    def project_own(j, carry):
        at = columns_of(j)
        product = jnp.dot(att[block:, :], w[:, at], preferred_element_type=jnp.float32)
        acc[:, at] = res[:, at].astype(jnp.float32) + gate[:, at] * (product + bias[:, at])
        return carry

    lax.fori_loop(0, tiles, project_own, 0)

    def finish(j, carry):
        at = columns_of(j)
        for c in range(parts):
            sum_copy(c, j).wait_recv()
        for c in range(parts):
            for origin in range(n_u):
                here = pl.ds(origin * rows + c * piece, piece)
                there = pl.ds(c * span + origin * piece, piece)
                mixed = acc[here, at] + gate[:, at] * received[there, at].astype(jnp.float32)
                result[here, at] = mixed.astype(jnp.bfloat16)
        out_copy(j).start()
        return carry

    lax.fori_loop(0, tiles, finish, 0)

    for copy in v_copies + k_copies + q_copies:
        copy.wait_send()
    for copies in part_copies + list(shared.values()) + list(forwarded.values()):
        for copy in copies:
            copy.wait_send()

    def drain(j, carry):
        for c in range(parts):
            sum_copy(c, j).wait_send()
        out_copy(j).wait()
        return carry

    lax.fori_loop(0, tiles, drain, 0)


def fused_shards(n_u, n_b, q, k, v, norm_query, norm_key, out_weight, out_bias, gate, residual):
    rows, features = q.shape[1:]
    depth, columns = out_weight.shape
    wide = features // (n_u * n_b)
    heads = wide // HEAD
    block = rows * n_u
    seq = block * n_b
    tiles = columns // (256 if columns % 256 == 0 else 128)
    chips = n_u // 2
    parts = 2
    bf16, f32 = jnp.bfloat16, jnp.float32
    dma = pltpu.SemaphoreType.DMA
    return pl.pallas_call(
        functools.partial(fused_kernel, n_u, parts),
        out_shape=jax.ShapeDtypeStruct(residual.shape, bf16),
        in_specs=[pl.BlockSpec(memory_space=pl.ANY)] * 9,
        out_specs=pl.BlockSpec(memory_space=pl.ANY),
        scratch_shapes=[
            pltpu.VMEM((rows, features), bf16),
            pltpu.VMEM((rows, features), bf16),
            pltpu.VMEM((1, features), f32),
            pltpu.VMEM((1, features), f32),
            pltpu.VMEM((depth, columns), bf16),
            pltpu.VMEM((columns,), f32),
            pltpu.VMEM((columns,), f32),
            pltpu.VMEM((block, columns), bf16),
            pltpu.VMEM((1, columns), f32),
            pltpu.VMEM((1, columns), f32),
            pltpu.VMEM((seq, wide), bf16),
            pltpu.VMEM((seq, wide), bf16),
            pltpu.VMEM((seq, wide), bf16),
            pltpu.VMEM((seq, depth), bf16),
            pltpu.VMEM((block, columns), f32),
            pltpu.VMEM((block, columns), bf16),
            pltpu.VMEM((block, columns), bf16),
            pltpu.VMEM((block, columns), bf16),
            dma((8,)),
            dma((3,)),
            dma((tiles,)),
            dma((3, 2 * n_u)),
            dma((3, 2 * n_u)),
            dma((parts, n_u)),
            dma((parts, n_u)),
            dma((parts + 1, chips)),
            dma((parts + 1, chips)),
            dma((parts + 1, max(chips - 1, 1))),
            dma((parts + 1, max(chips - 1, 1))),
            dma((parts, tiles)),
            dma((parts, tiles)),
        ],
        compiler_params=pltpu.CompilerParams(
            collective_id=0, has_side_effects=True, vmem_limit_bytes=63 * 1024 * 1024
        ),
    )(
        q, k, v,
        norm_query.reshape(1, features), norm_key.reshape(1, features),
        out_weight,
        out_bias, gate,
        residual,
    )


def normalize(rows_in, gain):
    wide = rows_in.astype(jnp.float32)
    factor = lax.rsqrt(jnp.mean(wide * wide, axis=-1, keepdims=True) + EPS)
    return (wide * factor * gain).astype(jnp.bfloat16)


def split_heads(array):
    return array.reshape(array.shape[0], array.shape[1] // HEAD, HEAD)


def initial_state(queries):
    count = queries.shape[1]
    length = queries.shape[0]
    return (
        jnp.full((count, length), -1e30, jnp.float32),
        jnp.zeros((count, length), jnp.float32),
        jnp.zeros((count, length, HEAD), jnp.float32),
    )


def absorb(state, keys, values, queries):
    peak, total, accum = state
    scores = jnp.einsum(
        "qhd,khd->hqk", queries, keys, preferred_element_type=jnp.float32
    ) * HEAD ** (-0.5)
    new_peak = jnp.maximum(peak, jnp.max(scores, axis=2))
    factor = jnp.exp(peak - new_peak)
    weights = jnp.exp(scores - new_peak[:, :, None])
    total = total * factor + jnp.sum(weights, axis=2)
    accum = accum * factor[:, :, None] + jnp.einsum(
        "hqk,khd->hqd", weights.astype(jnp.bfloat16), values, preferred_element_type=jnp.float32
    )
    return (new_peak, total, accum)


def attend_blocks(state, keys, values, queries):
    length = keys.shape[0]
    stride = 512
    count = keys.shape[1] // HEAD
    key_blocks = keys.reshape(length // stride, stride, count, HEAD)
    value_blocks = values.reshape(length // stride, stride, count, HEAD)

    def visit(carry, pair):
        return (absorb(carry, pair[0], pair[1], queries), None)

    state, unused = lax.scan(visit, state, (key_blocks, value_blocks))
    return state


def general_shards(
    query_rows, key_rows, value_rows, norm_query, norm_key, out_weight, out_bias, gate, residual
):
    local_query = normalize(query_rows[0], norm_query)
    local_key = normalize(key_rows[0], norm_key)
    local_value = value_rows[0]
    head_query = lax.all_to_all(local_query, "uly", split_axis=1, concat_axis=0, tiled=True)
    head_key, head_value = (
        lax.all_to_all(local_key, "uly", split_axis=1, concat_axis=0, tiled=True),
        lax.all_to_all(local_value, "uly", split_axis=1, concat_axis=0, tiled=True),
    )
    queries = split_heads(head_query)
    state = attend_blocks(
        initial_state(queries),
        lax.all_gather(head_key, "blk", axis=0, tiled=True),
        lax.all_gather(head_value, "blk", axis=0, tiled=True),
        queries,
    )
    peak, total, accum = state
    length = queries.shape[0]
    attended = (accum / total[:, :, None]).astype(jnp.bfloat16)
    attended = attended.transpose(1, 0, 2).reshape(length, queries.shape[1] * HEAD)
    gathered = lax.all_gather(attended, "uly", axis=1, tiled=True)
    projected = jnp.dot(
        gathered,
        lax.all_gather(out_weight, "blk", axis=0, tiled=True),
        preferred_element_type=jnp.float32,
    )
    mixed = residual[0].astype(jnp.float32) + gate * (projected + out_bias)
    return mixed.astype(jnp.bfloat16)[None]


def solution(mesh):
    n_u, n_b = mesh.shape["uly"], mesh.shape["blk"]
    placed = (
        P(("dp", "blk"), "uly", None),
        P(("dp", "blk"), "uly", None),
        P(("dp", "blk"), "uly", None),
        P(),
        P(),
        P("blk", "uly"),
        P("uly"),
        P("uly"),
        P(("dp", "blk"), None, "uly"),
    )

    def shards(query_rows, *rest):
        heads = query_rows.shape[2] // HEAD
        if n_b == 2 and n_u % 2 == 0 and heads % (n_u * n_b) == 0:
            return fused_shards(n_u, n_b, query_rows, *rest)
        return general_shards(query_rows, *rest)

    return jax.shard_map(
        shards, mesh=mesh, in_specs=placed, out_specs=P(("dp", "blk"), None, "uly"), check_vma=False
    )
```

```python
import functools

import jax
import jax.numpy as jnp
from jax import lax
from jax.experimental import pallas as pl
from jax.experimental.pallas import tpu as pltpu
from jax.sharding import PartitionSpec as P

HEAD = 128
EPS = 1e-06
MESH = pl.DeviceIdType.MESH
LOG2E = 1.4426950408889634


def normalize_rows(rows_ref, gain_ref):
    count = rows_ref.shape[0]
    step = 16

    def visit(i, carry):
        at = pl.ds(pl.multiple_of(i * step, step), step)
        wide = rows_ref[at, :].astype(jnp.float32)
        factor = lax.rsqrt(jnp.mean(wide * wide, axis=-1, keepdims=True) + EPS)
        rows_ref[at, :] = (wide * factor * gain_ref[...]).astype(jnp.bfloat16)
        return carry

    lax.fori_loop(0, count // step, visit, 0)


def fused_kernel(
    n_u, parts,
    q_hbm, k_hbm, v_hbm, nq_hbm, nk_hbm, w_hbm, bias_hbm, gate_hbm, res_hbm,
    out_hbm,
    q_in, k_in, nq, nk, w, bias_line, gate_line, res, bias, gate,
    q_all, k_all, v_all, att, acc, sent, received, result,
    load_sem, own_sem, out_sem, send_sem, recv_sem, q_send, q_recv, att_send, att_recv, fwd_send, fwd_recv, sum_send, sum_recv,
):
    u = lax.axis_index("uly")
    b = lax.axis_index("blk")
    other = 1 - b
    rows = q_in.shape[0]
    wide = q_all.shape[1]
    heads = wide // HEAD
    block = rows * n_u
    columns = w.shape[1]
    tile = 256 if columns % 256 == 0 else 128
    tiles = columns // tile
    sibling = u + 1 - 2 * lax.rem(u, 2)

    peers = [(1, du) for du in range(n_u)] + [(0, du) for du in range(1, n_u)]

    def peer_id(db, du):
        return {"uly": lax.rem(u + du, n_u), "blk": other if db else b}

    barrier = pltpu.get_barrier_semaphore()
    for db, du in peers:
        pl.semaphore_signal(barrier, inc=1, device_id=peer_id(db, du), device_id_type=MESH)

    loads = [
        pltpu.make_async_copy(source, target, load_sem.at[i])
        for i, (source, target) in enumerate(
            (
                (k_hbm.at[0], k_in),
                (nk_hbm, nk),
                (q_hbm.at[0], q_in),
                (nq_hbm, nq),
                (w_hbm, w),
                (bias_hbm, bias_line),
                (gate_hbm, gate_line),
                (res_hbm.at[0], res),
            )
        )
    ]
    for load in loads[:4]:
        load.start()

    def place_copy(source, target, db, du, first, count, at, send, recv):
        to = peer_id(db, du)
        start = pl.multiple_of((to["blk"] * n_u + to["uly"]) * wide, HEAD)
        copy = pltpu.make_async_remote_copy(
            src_ref=source.at[pl.ds(first, count), pl.ds(start, wide)],
            dst_ref=target.at[pl.ds(at, count), :],
            send_sem=send,
            recv_sem=recv,
            device_id=to,
            device_id_type=MESH,
        )
        copy.start()
        return copy

    def keep(index, source, target):
        copy = pltpu.make_async_copy(
            source.at[:, pl.ds(pl.multiple_of((b * n_u + u) * wide, HEAD), wide)],
            target.at[pl.ds(pl.multiple_of(block + u * rows, rows), rows), :],
            own_sem.at[index],
        )
        copy.start()
        return copy

    def spread(index, source, target, some):
        return [
            place_copy(
                source, target, db, du, 0, rows, pl.multiple_of((0 if db else block) + u * rows, rows),
                send_sem.at[index, db * n_u + du], recv_sem.at[index, db * n_u + du],
            )
            for db, du in some
        ]

    piece = rows // parts
    span = piece * n_u

    def spread_part(c):
        return [
            place_copy(
                q_in, q_all, 1, du, c * piece, piece, pl.multiple_of(c * span + u * piece, piece),
                q_send.at[c, du], q_recv.at[c, du],
            )
            for du in range(n_u)
        ]

    loads[0].wait()
    loads[1].wait()
    normalize_rows(k_in, nk)
    loads[2].wait()
    loads[3].wait()
    normalize_rows(q_in, nq)
    pl.semaphore_wait(barrier, len(peers))
    v_copies = spread(0, v_hbm.at[0], v_all, peers)
    v_mine = keep(0, v_hbm.at[0], v_all)
    k_copies = spread(1, k_in, k_all, peers)
    k_mine = keep(1, k_in, k_all)
    part_copies = [spread_part(0)]
    for load in loads[4:]:
        load.start()

    for copy in v_copies + k_copies:
        copy.wait_recv()
    v_mine.wait()
    k_mine.wait()
    for c in range(1, parts):
        part_copies.append(spread_part(c))

    scale = HEAD ** (-0.5) * LOG2E
    sections = [(c * span, span) for c in range(parts)] + [(block, block)]

    def attend(section):
        first, count = sections[section]
        for h in range(heads):
            feature = pl.ds(h * HEAD, HEAD)
            scores = lax.dot_general(
                q_all[pl.ds(first, count), feature],
                k_all[:, feature],
                (((1,), (1,)), ((), ())),
                preferred_element_type=jnp.float32,
            )
            peak = jnp.max(scores, axis=1, keepdims=True)
            weights = jnp.exp2((scores - peak) * scale)
            total = jnp.sum(weights, axis=1, keepdims=True)
            numer = jnp.dot(weights.astype(jnp.bfloat16), v_all[:, feature], preferred_element_type=jnp.float32)
            at = pl.multiple_of(u * wide + h * HEAD, HEAD)
            att[pl.ds(first, count), pl.ds(at, HEAD)] = (numer / total).astype(jnp.bfloat16)

    chips = n_u // 2
    pair = [2 * i for i in range(1, chips)]
    shared, forwarded = {}, {}

    def pass_on(section, origin, to, send, recv):
        first, count = sections[section]
        place = att.at[pl.ds(first, count), pl.ds(pl.multiple_of(origin * wide, HEAD), wide)]
        copy = pltpu.make_async_remote_copy(
            src_ref=place, dst_ref=place, send_sem=send, recv_sem=recv, device_id={"uly": to}, device_id_type=MESH
        )
        copy.start()
        return copy

    def share(section):
        shared[section] = [
            pass_on(section, u, to, att_send.at[section, i], att_recv.at[section, i])
            for i, to in enumerate([lax.rem(u + du, n_u) for du in pair] + [sibling])
        ]

    def gather(section):
        forwarded[section] = []
        for i, du in enumerate(pair):
            shared[section][i].wait_recv()
            origin = lax.rem(u + n_u - du, n_u)
            forwarded[section].append(
                pass_on(section, origin, sibling, fwd_send.at[section, i], fwd_recv.at[section, i])
            )
        shared[section][-1].wait_recv()
        for copy in forwarded[section]:
            copy.wait_recv()

    def columns_of(j):
        return pl.ds(pl.multiple_of(j * tile, tile), tile)

    def sum_copy(c, j):
        place = (pl.ds(c * span, span), columns_of(j))
        return pltpu.make_async_remote_copy(
            src_ref=sent.at[place],
            dst_ref=received.at[place],
            send_sem=sum_send.at[c, j],
            recv_sem=sum_recv.at[c, j],
            device_id={"blk": other},
            device_id_type=MESH,
        )

    def out_copy(j):
        return pltpu.make_async_copy(result.at[:, columns_of(j)], out_hbm.at[0, :, columns_of(j)], out_sem.at[j])

    def project_part(c):
        def visit(j, carry):
            product = jnp.dot(
                att[pl.ds(c * span, span), :], w[:, columns_of(j)], preferred_element_type=jnp.float32
            )
            sent[pl.ds(c * span, span), columns_of(j)] = product.astype(jnp.bfloat16)
            sum_copy(c, j).start()
            return carry

        lax.fori_loop(0, tiles, visit, 0)

    def attend_own():
        for copy in q_copies:
            copy.wait_recv()
        q_mine.wait()
        attend(parts)
        share(parts)

    for c in range(parts):
        for copy in part_copies[c]:
            copy.wait_recv()
        attend(c)
        share(c)

    q_copies = spread(2, q_in, q_all, peers[n_u:])
    q_mine = keep(2, q_in, q_all)

    for load in loads[4:]:
        load.wait()
    bias[...] = bias_line[...].reshape(1, columns)
    gate[...] = gate_line[...].reshape(1, columns)

    for c in range(parts):
        gather(c)
        project_part(c)
        if c == parts - 1:
            attend_own()
    gather(parts)

    def project_own(j, carry):
        at = columns_of(j)
        product = jnp.dot(att[block:, :], w[:, at], preferred_element_type=jnp.float32)
        acc[:, at] = res[:, at].astype(jnp.float32) + gate[:, at] * (product + bias[:, at])
        return carry

    lax.fori_loop(0, tiles, project_own, 0)

    def finish(j, carry):
        at = columns_of(j)
        for c in range(parts):
            sum_copy(c, j).wait_recv()
        for c in range(parts):
            for origin in range(n_u):
                here = pl.ds(origin * rows + c * piece, piece)
                there = pl.ds(c * span + origin * piece, piece)
                mixed = acc[here, at] + gate[:, at] * received[there, at].astype(jnp.float32)
                result[here, at] = mixed.astype(jnp.bfloat16)
        out_copy(j).start()
        return carry

    lax.fori_loop(0, tiles, finish, 0)

    for copy in v_copies + k_copies + q_copies:
        copy.wait_send()
    for copies in part_copies + list(shared.values()) + list(forwarded.values()):
        for copy in copies:
            copy.wait_send()

    def drain(j, carry):
        for c in range(parts):
            sum_copy(c, j).wait_send()
        out_copy(j).wait()
        return carry

    lax.fori_loop(0, tiles, drain, 0)


def fused_shards(n_u, n_b, q, k, v, norm_query, norm_key, out_weight, out_bias, gate, residual):
    rows, features = q.shape[1:]
    depth, columns = out_weight.shape
    wide = features // (n_u * n_b)
    heads = wide // HEAD
    block = rows * n_u
    seq = block * n_b
    tiles = columns // (256 if columns % 256 == 0 else 128)
    chips = n_u // 2
    parts = 2
    bf16, f32 = jnp.bfloat16, jnp.float32
    dma = pltpu.SemaphoreType.DMA
    return pl.pallas_call(
        functools.partial(fused_kernel, n_u, parts),
        out_shape=jax.ShapeDtypeStruct(residual.shape, bf16),
        in_specs=[pl.BlockSpec(memory_space=pl.ANY)] * 9,
        out_specs=pl.BlockSpec(memory_space=pl.ANY),
        scratch_shapes=[
            pltpu.VMEM((rows, features), bf16),
            pltpu.VMEM((rows, features), bf16),
            pltpu.VMEM((1, features), f32),
            pltpu.VMEM((1, features), f32),
            pltpu.VMEM((depth, columns), bf16),
            pltpu.VMEM((columns,), f32),
            pltpu.VMEM((columns,), f32),
            pltpu.VMEM((block, columns), bf16),
            pltpu.VMEM((1, columns), f32),
            pltpu.VMEM((1, columns), f32),
            pltpu.VMEM((seq, wide), bf16),
            pltpu.VMEM((seq, wide), bf16),
            pltpu.VMEM((seq, wide), bf16),
            pltpu.VMEM((seq, depth), bf16),
            pltpu.VMEM((block, columns), f32),
            pltpu.VMEM((block, columns), bf16),
            pltpu.VMEM((block, columns), bf16),
            pltpu.VMEM((block, columns), bf16),
            dma((8,)),
            dma((3,)),
            dma((tiles,)),
            dma((3, 2 * n_u)),
            dma((3, 2 * n_u)),
            dma((parts, n_u)),
            dma((parts, n_u)),
            dma((parts + 1, chips)),
            dma((parts + 1, chips)),
            dma((parts + 1, max(chips - 1, 1))),
            dma((parts + 1, max(chips - 1, 1))),
            dma((parts, tiles)),
            dma((parts, tiles)),
        ],
        compiler_params=pltpu.CompilerParams(
            collective_id=0, has_side_effects=True, vmem_limit_bytes=63 * 1024 * 1024
        ),
    )(
        q, k, v,
        norm_query.reshape(1, features), norm_key.reshape(1, features),
        out_weight,
        out_bias, gate,
        residual,
    )


def normalize(rows_in, gain):
    wide = rows_in.astype(jnp.float32)
    factor = lax.rsqrt(jnp.mean(wide * wide, axis=-1, keepdims=True) + EPS)
    return (wide * factor * gain).astype(jnp.bfloat16)


def split_heads(array):
    return array.reshape(array.shape[0], array.shape[1] // HEAD, HEAD)


def initial_state(queries):
    count = queries.shape[1]
    length = queries.shape[0]
    return (
        jnp.full((count, length), -1e30, jnp.float32),
        jnp.zeros((count, length), jnp.float32),
        jnp.zeros((count, length, HEAD), jnp.float32),
    )


def absorb(state, keys, values, queries):
    peak, total, accum = state
    scores = jnp.einsum(
        "qhd,khd->hqk", queries, keys, preferred_element_type=jnp.float32
    ) * HEAD ** (-0.5)
    new_peak = jnp.maximum(peak, jnp.max(scores, axis=2))
    factor = jnp.exp(peak - new_peak)
    weights = jnp.exp(scores - new_peak[:, :, None])
    total = total * factor + jnp.sum(weights, axis=2)
    accum = accum * factor[:, :, None] + jnp.einsum(
        "hqk,khd->hqd", weights.astype(jnp.bfloat16), values, preferred_element_type=jnp.float32
    )
    return (new_peak, total, accum)


def attend_blocks(state, keys, values, queries):
    length = keys.shape[0]
    stride = 512
    count = keys.shape[1] // HEAD
    key_blocks = keys.reshape(length // stride, stride, count, HEAD)
    value_blocks = values.reshape(length // stride, stride, count, HEAD)

    def visit(carry, pair):
        return (absorb(carry, pair[0], pair[1], queries), None)

    state, unused = lax.scan(visit, state, (key_blocks, value_blocks))
    return state


def general_shards(
    query_rows, key_rows, value_rows, norm_query, norm_key, out_weight, out_bias, gate, residual
):
    local_query = normalize(query_rows[0], norm_query)
    local_key = normalize(key_rows[0], norm_key)
    local_value = value_rows[0]
    head_query = lax.all_to_all(local_query, "uly", split_axis=1, concat_axis=0, tiled=True)
    head_key, head_value = (
        lax.all_to_all(local_key, "uly", split_axis=1, concat_axis=0, tiled=True),
        lax.all_to_all(local_value, "uly", split_axis=1, concat_axis=0, tiled=True),
    )
    queries = split_heads(head_query)
    state = attend_blocks(
        initial_state(queries),
        lax.all_gather(head_key, "blk", axis=0, tiled=True),
        lax.all_gather(head_value, "blk", axis=0, tiled=True),
        queries,
    )
    peak, total, accum = state
    length = queries.shape[0]
    attended = (accum / total[:, :, None]).astype(jnp.bfloat16)
    attended = attended.transpose(1, 0, 2).reshape(length, queries.shape[1] * HEAD)
    gathered = lax.all_gather(attended, "uly", axis=1, tiled=True)
    projected = jnp.dot(
        gathered,
        lax.all_gather(out_weight, "blk", axis=0, tiled=True),
        preferred_element_type=jnp.float32,
    )
    mixed = residual[0].astype(jnp.float32) + gate * (projected + out_bias)
    return mixed.astype(jnp.bfloat16)[None]


def solution(mesh):
    n_u, n_b = mesh.shape["uly"], mesh.shape["blk"]
    placed = (
        P(("dp", "blk"), "uly", None),
        P(("dp", "blk"), "uly", None),
        P(("dp", "blk"), "uly", None),
        P(),
        P(),
        P("blk", "uly"),
        P("uly"),
        P("uly"),
        P(("dp", "blk"), None, "uly"),
    )

    def shards(query_rows, *rest):
        heads = query_rows.shape[2] // HEAD
        if n_b == 2 and n_u % 2 == 0 and heads % (n_u * n_b) == 0:
            return fused_shards(n_u, n_b, query_rows, *rest)
        return general_shards(query_rows, *rest)

    return jax.shard_map(
        shards, mesh=mesh, in_specs=placed, out_specs=P(("dp", "blk"), None, "uly"), check_vma=False
    )
```
